32 devices in a mesh: grp: 2 (over y), gx: 4 (over z), gy: 2 (over x), gz: 2 (over core).
Axes of the slice: x: 2, y: 2, z: 4, core: 2. Of those that a mesh axis runs over, the one named last changes fastest.
Arguments:
- tokens: bfloat16 [128, 6144], P(('grp', 'gx'), ('gy', 'gz')), parts along dimension 0, may hold values from -6 to 6
- w_gate: bfloat16 [6144, 14336], P(('gy', 'gz'), 'gx'), may hold values from -0.078125 to 0.078125
- w_up: bfloat16 [6144, 14336], P(('gy', 'gz'), 'gx'), may hold values from -0.078125 to 0.078125
- w_down: bfloat16 [14336, 6144], P('gx', ('gy', 'gz')), may hold values from -0.046875 to 0.046875
- grad_out: bfloat16 [128, 6144], P(('grp', 'gx'), ('gy', 'gz')), parts along dimension 0, may hold values from -2.5 to 2.5
Outputs:
- mixed: bfloat16 [128, 6144], P(('grp', 'gx'), ('gy', 'gz')), parts along dimension 0
- grad_tokens: bfloat16 [128, 6144], P(('grp', 'gx'), ('gy', 'gz')), parts along dimension 0
- grad_gate: bfloat16 [12288, 14336], P(('grp', 'gy', 'gz'), 'gx'), parts along dimension 0
- grad_up: bfloat16 [12288, 14336], P(('grp', 'gy', 'gz'), 'gx'), parts along dimension 0
- grad_down: bfloat16 [28672, 6144], P(('grp', 'gx'), ('gy', 'gz')), parts along dimension 0
The draws below stay inside these ranges and needn't reach their ends.
There are 2 independent parts, one for each index of `grp`. The reference program is written for one: setup_inputs(seed, part) draws one part's arguments, and reference() takes and returns one part's arrays. A program takes and returns all parts, laid end to end along the dimension named above; an argument that names none is the same for every part. Nothing has to cross between parts.
All inputs are finite; a program needn't handle non-finite values.
Results may differ from the reference program's by a relative error of at most 0.0051.
Values may be sent and summed in bfloat16 or wider, within the bound.
A program may use at most 192 MiB of HBM per device.

```python
import jax
import jax.numpy as jnp

D = 6144
FF = 14336
TOKENS = 64


def levels(rng, shape, pieces, low, top_value):
    def one(axis_at, blocks):
        steps = jax.random.uniform(jax.random.fold_in(jax.random.fold_in(rng, 6), axis_at), (blocks,), jnp.float32, low / len(pieces), top_value / len(pieces))
        return jnp.repeat(jnp.exp(steps), shape[axis_at] // blocks).reshape((-1,) + (1,) * (len(shape) - axis_at - 1))

    gain = one(*pieces[0])
    for cut in pieces[1:]:
        gain = gain * one(*cut)
    return gain


def gaussian(own_key, dims, width, reach, pieces=(), held_as=jnp.bfloat16):
    drawn = jax.random.normal(own_key, dims, jnp.float32) * width
    if len(pieces) > 0:
        drawn = levels(own_key, dims, pieces, -0.22, 0.18) * drawn
    return jnp.clip(drawn, min=-reach, max=reach).astype(held_as)


def setup_inputs(seed: int = 0, part: int = 0) -> dict:
    arg_keys = jax.random.split(jax.random.key(seed), 6)
    part_splits = jax.random.split(jax.random.fold_in(arg_keys[5], part), 6)
    return {
        "tokens": gaussian(part_splits[0], (TOKENS, D), 1.0, 6.0, ((0, 4), (1, 4))),
        "w_gate": gaussian(arg_keys[1], (D, FF), D ** -0.5, 0.078125, ((0, 4), (1, 4))),
        "w_up": gaussian(arg_keys[2], (D, FF), D ** -0.5, 0.078125, ((0, 4), (1, 4))),
        "w_down": gaussian(arg_keys[3], (FF, D), FF ** -0.5, 0.046875, ((0, 4), (1, 4))),
        "grad_out": gaussian(part_splits[4], (TOKENS, D), 0.25, 2.5, ((0, 4), (1, 4))),
    }


def gate_slope(gate_pre):
    sig = jax.nn.sigmoid(gate_pre)
    return sig * (1.0 + gate_pre * (1.0 - sig))


def reference(tokens, w_gate, w_up, w_down, grad_out):
    gate_pre = jnp.dot(tokens, w_gate, preferred_element_type=jnp.float32)
    up_pre = jnp.dot(tokens, w_up, preferred_element_type=jnp.float32)
    act_gate = jax.nn.silu(gate_pre)
    hidden = (act_gate * up_pre).astype(jnp.bfloat16)
    mixed = jnp.dot(hidden, w_down, preferred_element_type=jnp.float32).astype(jnp.bfloat16)
    grad_hidden = jnp.dot(grad_out, w_down.T, preferred_element_type=jnp.float32)
    pre_gate = (grad_hidden * up_pre * gate_slope(gate_pre)).astype(jnp.bfloat16)
    pre_up = (grad_hidden * act_gate).astype(jnp.bfloat16)
    grad_down = jnp.dot(hidden.T, grad_out, preferred_element_type=jnp.float32).astype(jnp.bfloat16)
    grad_gate = jnp.dot(tokens.T, pre_gate, preferred_element_type=jnp.float32).astype(jnp.bfloat16)
    grad_up = jnp.dot(tokens.T, pre_up, preferred_element_type=jnp.float32).astype(jnp.bfloat16)
    back = jnp.dot(pre_gate, w_gate.T, preferred_element_type=jnp.float32)
    back = back + jnp.dot(pre_up, w_up.T, preferred_element_type=jnp.float32)
    return mixed, back.astype(jnp.bfloat16), grad_gate, grad_up, grad_down
```

```python
import functools

import jax
import jax.numpy as jnp
from jax import lax
from jax.experimental import pallas as pl
from jax.experimental.pallas import tpu as pltpu
from jax.sharding import PartitionSpec as P

MESH = pl.DeviceIdType.MESH
BF16 = jnp.bfloat16
F32 = jnp.float32
VMEM_BYTES = 58 * 2**20


def dot(left, right, dims=((1,), (0,))):
    return lax.dot_general(left, right, (dims, ((), ())), preferred_element_type=F32)


def chunk_of(width):
    return 512 if width % 512 == 0 else width


def remote(src, dst, send_sem, recv_sem, device):
    return pltpu.make_async_remote_copy(
        src_ref=src,
        dst_ref=dst,
        send_sem=send_sem,
        recv_sem=recv_sem,
        device_id=device,
        device_id_type=MESH,
    )


def main_kernel(
    n,
    m,
    tok_ref,
    cot_ref,
    wg_hbm,
    wu_hbm,
    wd_hbm,
    mixed_ref,
    gtok_ref,
    acts_ref,
    rows_ref,
    rows,
    wg,
    wu,
    wd,
    part,
    own,
    core_out,
    core_in,
    chip_out,
    chip_in,
    acts,
    mixed_acc,
    gtok_acc,
    scat_out,
    scat_in,
    w_sem,
    gather_send,
    gather_recv,
    core_send,
    core_recv,
    chip_send,
    chip_recv,
    acts_send,
    acts_recv,
    scat_send,
    scat_recv,
):
    me_x, me_y, me_z = (lax.axis_index(a) for a in ("gx", "gy", "gz"))
    other = 1 - me_z
    steps, depth, width = wg.shape
    block = tok_ref.shape[0]
    half = (n * block) // 2
    mine = pl.ds(pl.multiple_of(me_z * half, half), half)
    theirs = pl.ds(pl.multiple_of(other * half, half), half)

    def slab(index):
        return pl.ds(pl.multiple_of(index * block, block), block)

    def weight_copies(k):
        columns = pl.ds(pl.multiple_of(k * width, width), width)
        if steps == 1:
            columns = slice(None)
        return (
            pltpu.make_async_copy(wg_hbm.at[:, columns], wg.at[k], w_sem.at[k, 0]),
            pltpu.make_async_copy(wu_hbm.at[:, columns], wu.at[k], w_sem.at[k, 1]),
            pltpu.make_async_copy(wd_hbm.at[columns, :], wd.at[k], w_sem.at[k, 2]),
        )

    for k in range(steps):
        for copy in weight_copies(k):
            copy.start()

    barrier = pltpu.get_barrier_semaphore()
    for d in range(1, n):
        pl.semaphore_signal(
            barrier, inc=1, device_id={"gx": lax.rem(me_x + d, n)}, device_id_type=MESH
        )
    for d in range(1, m):
        pl.semaphore_signal(
            barrier, inc=1, device_id={"gy": lax.rem(me_y + d, m)}, device_id_type=MESH
        )
    pl.semaphore_signal(barrier, inc=1, device_id={"gz": other}, device_id_type=MESH)
    pl.semaphore_wait(barrier, n + m - 1)

    def gather_copy(a, d):
        src = tok_ref if a == 0 else cot_ref
        return remote(
            src,
            rows.at[a, slab(me_x)],
            gather_send.at[a, d],
            gather_recv.at[a, d],
            {"gx": lax.rem(me_x + d, n)},
        )

    for a in range(2):
        for d in range(1, n):
            gather_copy(a, d).start()
    rows[0, slab(me_x)] = tok_ref[...]
    rows[1, slab(me_x)] = cot_ref[...]
    mixed_acc[...] = jnp.zeros_like(mixed_acc)
    gtok_acc[...] = jnp.zeros_like(gtok_acc)
    for a in range(2):
        for d in range(1, n):
            gather_copy(a, d).wait()
    rows_ref[...] = rows[...]

    def core_copy(k):
        return remote(
            core_out.at[k], core_in.at[k], core_send.at[k], core_recv.at[k], {"gz": other}
        )

    def chip_copy(k, d):
        return remote(
            chip_out.at[k],
            chip_in.at[k, d - 1],
            chip_send.at[k, d],
            chip_recv.at[k, d],
            {"gy": lax.rem(me_y + d, m)},
        )

    def acts_copy(k):
        return remote(
            acts.at[k, :, mine],
            acts.at[k, :, mine],
            acts_send.at[k],
            acts_recv.at[k],
            {"gz": other},
        )

    def project(k):
        for copy in weight_copies(k):
            copy.wait()
        part[0] = dot(rows[0], wg[k])
        part[1] = dot(rows[0], wu[k])
        part[2] = dot(rows[1], wd[k], ((1,), (1,)))
        core_out[k] = part[:, theirs].astype(BF16)
        core_copy(k).start()
        own[k] = part[:, mine]

    def sum_cores(k):
        core_copy(k).wait()
        own[k] = own[k] + core_in[k].astype(F32)
        chip_out[k] = own[k].astype(BF16)
        for d in range(1, m):
            chip_copy(k, d).start()

    def activate(k):
        for d in range(1, m):
            chip_copy(k, d).wait()
        total = []
        for i in range(3):
            value = own[k, i]
            for d in range(1, m):
                value = value + chip_in[k, d - 1, i].astype(F32)
            total.append(value)
        gate, up, grad = total
        sig = jax.nn.sigmoid(gate)
        act = gate * sig
        acts[k, 0, mine] = (act * up).astype(BF16)
        acts[k, 1, mine] = (grad * up * (sig * (1.0 + gate * (1.0 - sig)))).astype(BF16)
        acts[k, 2, mine] = (grad * act).astype(BF16)
        acts_copy(k).start()

    tile = chunk_of(depth)

    def contract(k):
        acts_copy(k).wait()
        acts_ref[k] = acts[k]
        for t in range(0, depth, tile):
            span = slice(t, t + tile)
            mixed_acc[:, span] += dot(acts[k, 0], wd[k, :, span])
            gtok_acc[:, span] += dot(acts[k, 1], wg[k, span, :], ((1,), (1,)))
            gtok_acc[:, span] += dot(acts[k, 2], wu[k, span, :], ((1,), (1,)))

    def step(i, carry):
        for lag, stage in ((0, project), (1, sum_cores), (2, activate), (3, contract)):
            @pl.when(jnp.logical_and(i >= lag, i < steps + lag))
            def _():
                stage(i - lag)

        return carry

    lax.fori_loop(0, steps + 3, step, 0)

    def scatter_copy(d):
        return remote(
            scat_out.at[d],
            scat_in.at[d],
            scat_send.at[d],
            scat_recv.at[d],
            {"gx": lax.rem(me_x + d, n)},
        )

    for d in range(1, n):
        peer = slab(lax.rem(me_x + d, n))
        scat_out[d, 0] = mixed_acc[peer].astype(BF16)
        scat_out[d, 1] = gtok_acc[peer].astype(BF16)
        scatter_copy(d).start()
    mixed_sum = mixed_acc[slab(me_x)]
    gtok_sum = gtok_acc[slab(me_x)]
    for d in range(1, n):
        scatter_copy(d).wait()
        mixed_sum = mixed_sum + scat_in[d, 0].astype(F32)
        gtok_sum = gtok_sum + scat_in[d, 1].astype(F32)
    mixed_ref[...] = mixed_sum.astype(BF16)
    gtok_ref[...] = gtok_sum.astype(BF16)


def outer_kernel(acts_ref, rows_ref, gg_ref, gu_ref, gd_ref, tok_t):
    @pl.when(pl.program_id(0) == 0)
    def _():
        tok_t[...] = rows_ref[0].T

    depth, width = gg_ref.shape
    tile = 256 if depth % 256 == 0 else depth

    def body(t, carry):
        span = pl.ds(pl.multiple_of(t * tile, tile), tile)
        left = tok_t[span, :]
        gg_ref[span, :] = dot(left, acts_ref[0, 1]).astype(BF16)
        gu_ref[span, :] = dot(left, acts_ref[0, 2]).astype(BF16)
        gd_ref[:, span] = dot(acts_ref[0, 0], rows_ref[1, :, span], ((0,), (0,))).astype(BF16)
        return carry

    lax.fori_loop(0, depth // tile, body, 0)


def local(n, m, tokens, w_gate, w_up, w_down, grad_out):
    block, depth = tokens.shape
    ff = w_gate.shape[1]
    width = chunk_of(ff)
    steps = ff // width
    count = n * block
    half = count // 2
    vmem = pl.BlockSpec(memory_space=pltpu.VMEM)
    anywhere = pl.BlockSpec(memory_space=pl.ANY)
    dma = pltpu.SemaphoreType.DMA
    mixed, gtok, acts, rows = pl.pallas_call(
        functools.partial(main_kernel, n, m),
        out_shape=(
            jax.ShapeDtypeStruct((block, depth), BF16),
            jax.ShapeDtypeStruct((block, depth), BF16),
            jax.ShapeDtypeStruct((steps, 3, count, width), BF16),
            jax.ShapeDtypeStruct((2, count, depth), BF16),
        ),
        in_specs=[vmem, vmem, anywhere, anywhere, anywhere],
        out_specs=(vmem, vmem, vmem, vmem),
        scratch_shapes=[
            pltpu.VMEM((2, count, depth), BF16),
            pltpu.VMEM((steps, depth, width), BF16),
            pltpu.VMEM((steps, depth, width), BF16),
            pltpu.VMEM((steps, width, depth), BF16),
            pltpu.VMEM((3, count, width), F32),
            pltpu.VMEM((steps, 3, half, width), F32),
            pltpu.VMEM((steps, 3, half, width), BF16),
            pltpu.VMEM((steps, 3, half, width), BF16),
            pltpu.VMEM((steps, 3, half, width), BF16),
            pltpu.VMEM((steps, m - 1, 3, half, width), BF16),
            pltpu.VMEM((steps, 3, count, width), BF16),
            pltpu.VMEM((count, depth), F32),
            pltpu.VMEM((count, depth), F32),
            pltpu.VMEM((n, 2, block, depth), BF16),
            pltpu.VMEM((n, 2, block, depth), BF16),
            dma((steps, 3)),
            dma((2, n)),
            dma((2, n)),
            dma((steps,)),
            dma((steps,)),
            dma((steps, m)),
            dma((steps, m)),
            dma((steps,)),
            dma((steps,)),
            dma((n,)),
            dma((n,)),
        ],
        compiler_params=pltpu.CompilerParams(
            collective_id=0, has_side_effects=True, vmem_limit_bytes=VMEM_BYTES
        ),
    )(tokens, grad_out, w_gate, w_up, w_down)
    grad_gate, grad_up, grad_down = pl.pallas_call(
        outer_kernel,
        grid=(steps,),
        out_shape=(
            jax.ShapeDtypeStruct((depth, ff), BF16),
            jax.ShapeDtypeStruct((depth, ff), BF16),
            jax.ShapeDtypeStruct((ff, depth), BF16),
        ),
        in_specs=[
            pl.BlockSpec((1, 3, count, width), lambda k: (k, 0, 0, 0)),
            pl.BlockSpec((2, count, depth), lambda k: (0, 0, 0)),
        ],
        out_specs=(
            pl.BlockSpec((depth, width), lambda k: (0, k)),
            pl.BlockSpec((depth, width), lambda k: (0, k)),
            pl.BlockSpec((width, depth), lambda k: (k, 0)),
        ),
        scratch_shapes=[pltpu.VMEM((depth, count), BF16)],
        compiler_params=pltpu.CompilerParams(vmem_limit_bytes=VMEM_BYTES),
    )(acts, rows)
    return mixed, gtok, grad_gate, grad_up, grad_down


def solution(mesh):
    return jax.shard_map(
        functools.partial(local, mesh.shape["gx"], mesh.shape["gy"]),
        mesh=mesh,
        in_specs=(
            P(("grp", "gx"), ("gy", "gz")),
            P(("gy", "gz"), "gx"),
            P(("gy", "gz"), "gx"),
            P("gx", ("gy", "gz")),
            P(("grp", "gx"), ("gy", "gz")),
        ),
        out_specs=(
            P(("grp", "gx"), ("gy", "gz")),
            P(("grp", "gx"), ("gy", "gz")),
            P(("grp", "gy", "gz"), "gx"),
            P(("grp", "gy", "gz"), "gx"),
            P(("grp", "gx"), ("gy", "gz")),
        ),
        check_vma=False,
    )
```

```python
import functools

import jax
import jax.numpy as jnp
from jax import lax
from jax.experimental import pallas as pl
from jax.experimental.pallas import tpu as pltpu
from jax.sharding import PartitionSpec as P

MESH = pl.DeviceIdType.MESH
BF16 = jnp.bfloat16
F32 = jnp.float32
VMEM_BYTES = 58 * 2**20


def dot(left, right, dims=((1,), (0,))):
    return lax.dot_general(left, right, (dims, ((), ())), preferred_element_type=F32)


def chunk_of(width):
    return 512 if width % 512 == 0 else width


def remote(src, dst, send_sem, recv_sem, device):
    return pltpu.make_async_remote_copy(
        src_ref=src,
        dst_ref=dst,
        send_sem=send_sem,
        recv_sem=recv_sem,
        device_id=device,
        device_id_type=MESH,
    )


def main_kernel(
    n,
    m,
    tok_ref,
    cot_ref,
    wg_hbm,
    wu_hbm,
    wd_hbm,
    mixed_ref,
    gtok_ref,
    acts_ref,
    rows_ref,
    rows,
    wg,
    wu,
    wd,
    part,
    own,
    core_out,
    core_in,
    chip_out,
    chip_in,
    acts,
    mixed_acc,
    gtok_acc,
    scat_out,
    scat_in,
    w_sem,
    gather_send,
    gather_recv,
    core_send,
    core_recv,
    chip_send,
    chip_recv,
    acts_send,
    acts_recv,
    scat_send,
    scat_recv,
):
    me_x, me_y, me_z = (lax.axis_index(a) for a in ("gx", "gy", "gz"))
    other = 1 - me_z
    steps, depth, width = wg.shape
    block = tok_ref.shape[0]
    half = (n * block) // 2
    mine = pl.ds(pl.multiple_of(me_z * half, half), half)
    theirs = pl.ds(pl.multiple_of(other * half, half), half)

    def slab(index):
        return pl.ds(pl.multiple_of(index * block, block), block)

    def weight_copies(k):
        columns = pl.ds(pl.multiple_of(k * width, width), width)
        if steps == 1:
            columns = slice(None)
        return (
            pltpu.make_async_copy(wg_hbm.at[:, columns], wg.at[k], w_sem.at[k, 0]),
            pltpu.make_async_copy(wu_hbm.at[:, columns], wu.at[k], w_sem.at[k, 1]),
            pltpu.make_async_copy(wd_hbm.at[columns, :], wd.at[k], w_sem.at[k, 2]),
        )

    for k in range(steps):
        for copy in weight_copies(k):
            copy.start()

    barrier = pltpu.get_barrier_semaphore()
    for d in range(1, n):
        pl.semaphore_signal(
            barrier, inc=1, device_id={"gx": lax.rem(me_x + d, n)}, device_id_type=MESH
        )
    for d in range(1, m):
        pl.semaphore_signal(
            barrier, inc=1, device_id={"gy": lax.rem(me_y + d, m)}, device_id_type=MESH
        )
    pl.semaphore_signal(barrier, inc=1, device_id={"gz": other}, device_id_type=MESH)
    pl.semaphore_wait(barrier, n + m - 1)

    def gather_copy(a, d):
        src = tok_ref if a == 0 else cot_ref
        return remote(
            src,
            rows.at[a, slab(me_x)],
            gather_send.at[a, d],
            gather_recv.at[a, d],
            {"gx": lax.rem(me_x + d, n)},
        )

    def gather_start(a):
        for d in range(1, n):
            gather_copy(a, d).start()

    def gather_wait(a):
        for d in range(1, n):
            gather_copy(a, d).wait()

    gather_start(0)
    rows[0, slab(me_x)] = tok_ref[...]
    rows[1, slab(me_x)] = cot_ref[...]
    mixed_acc[...] = jnp.zeros_like(mixed_acc)
    gtok_acc[...] = jnp.zeros_like(gtok_acc)
    gather_wait(0)
    gather_start(1)

    parts = (slice(0, 2), slice(2, 3))
    results = (slice(0, 1), slice(1, 3))

    def core_copy(k, way):
        return remote(
            core_out.at[k, parts[way]],
            core_in.at[k, parts[way]],
            core_send.at[k, way],
            core_recv.at[k, way],
            {"gz": other},
        )

    def chip_copy(k, way, d):
        return remote(
            chip_out.at[k, parts[way]],
            chip_in.at[k, d - 1, parts[way]],
            chip_send.at[k, d, way],
            chip_recv.at[k, d, way],
            {"gy": lax.rem(me_y + d, m)},
        )

    def acts_copy(k, way):
        half_acts = acts.at[k, results[way], mine]
        return remote(
            half_acts, half_acts, acts_send.at[k, way], acts_recv.at[k, way], {"gz": other}
        )

    def send_partial(k, way):
        span = parts[way]
        core_out[k, span] = part[span, theirs].astype(BF16)
        core_copy(k, way).start()
        own[k, span] = part[span, mine]

    def project(k):
        gate_copy, up_copy, _ = weight_copies(k)
        gate_copy.wait()
        part[0] = dot(rows[0], wg[k])
        up_copy.wait()
        part[1] = dot(rows[0], wu[k])
        send_partial(k, 0)

    def project_back(k):
        @pl.when(k == 0)
        def _():
            gather_wait(1)

        weight_copies(k)[2].wait()
        part[2] = dot(rows[1], wd[k], ((1,), (1,)))
        send_partial(k, 1)

    def sum_cores(k, way):
        span = parts[way]
        core_copy(k, way).wait()
        total = own[k, span] + core_in[k, span].astype(F32)
        own[k, span] = total
        chip_out[k, span] = total.astype(BF16)
        for d in range(1, m):
            chip_copy(k, way, d).start()

    def sum_chips(k, way):
        span = parts[way]
        total = own[k, span]
        for d in range(1, m):
            chip_copy(k, way, d).wait()
            total = total + chip_in[k, d - 1, span].astype(F32)
        return total

    def activate(k):
        total = sum_chips(k, 0)
        own[k, parts[0]] = total
        gate, up = total[0], total[1]
        acts[k, 0, mine] = (gate * jax.nn.sigmoid(gate) * up).astype(BF16)
        acts_copy(k, 0).start()

    def activate_back(k):
        grad = sum_chips(k, 1)[0]
        gate, up = own[k, 0], own[k, 1]
        sig = jax.nn.sigmoid(gate)
        acts[k, 1, mine] = (grad * up * (sig * (1.0 + gate * (1.0 - sig)))).astype(BF16)
        acts[k, 2, mine] = (grad * (gate * sig)).astype(BF16)
        acts_copy(k, 1).start()

    def scatter_copy(d, a):
        return remote(
            scat_out.at[d, a],
            scat_in.at[d, a],
            scat_send.at[d, a],
            scat_recv.at[d, a],
            {"gx": lax.rem(me_x + d, n)},
        )

    def scatter(a, acc):
        for d in range(1, n):
            scat_out[d, a] = acc[slab(lax.rem(me_x + d, n))].astype(BF16)
            scatter_copy(d, a).start()

    def collect(a, acc, out_ref):
        total = acc[slab(me_x)]
        for d in range(1, n):
            scatter_copy(d, a).wait()
            total = total + scat_in[d, a].astype(F32)
        out_ref[...] = total.astype(BF16)

    tile = chunk_of(depth)

    def contract(k):
        acts_copy(k, 0).wait()
        for t in range(0, depth, tile):
            span = slice(t, t + tile)
            mixed_acc[:, span] += dot(acts[k, 0], wd[k, :, span])

        @pl.when(k == steps - 1)
        def _():
            scatter(0, mixed_acc)

    def contract_back(k):
        acts_copy(k, 1).wait()
        acts_ref[k] = acts[k]
        for t in range(0, depth, tile):
            span = slice(t, t + tile)
            gtok_acc[:, span] += dot(acts[k, 1], wg[k, span, :], ((1,), (1,))) + dot(
                acts[k, 2], wu[k, span, :], ((1,), (1,))
            )

    stages = (
        (0, project),
        (1, lambda k: sum_cores(k, 0)),
        (4, activate),
        (6, contract),
        (3, project_back),
        (4, lambda k: sum_cores(k, 1)),
        (7, activate_back),
        (9, contract_back),
    )

    def step(i, carry):
        for lag, stage in stages:
            @pl.when(jnp.logical_and(i >= lag, i < steps + lag))
            def _():
                stage(i - lag)

        return carry

    lax.fori_loop(0, steps + 9, step, 0)

    scatter(1, gtok_acc)
    rows_ref[...] = rows[...]
    collect(0, mixed_acc, mixed_ref)
    collect(1, gtok_acc, gtok_ref)


def outer_kernel(
    acts_ref, rows_ref, mixed_in, gtok_in, mixed_ref, gtok_ref, gg_ref, gu_ref, gd_ref, tok_t, hid_t
):
    @pl.when(pl.program_id(0) == 0)
    def _():
        tok_t[...] = rows_ref[0].T
        mixed_ref[...] = mixed_in[...]
        gtok_ref[...] = gtok_in[...]

    depth, width = gg_ref.shape
    hid_t[...] = acts_ref[0, 0].T
    tile = 256 if depth % 256 == 0 else depth
    for t in range(0, depth, tile):
        span = slice(t, t + tile)
        gg_ref[span, :] = dot(tok_t[span, :], acts_ref[0, 1]).astype(BF16)
        gu_ref[span, :] = dot(tok_t[span, :], acts_ref[0, 2]).astype(BF16)
    tile = 128 if width % 128 == 0 else width
    for t in range(0, width, tile):
        span = slice(t, t + tile)
        gd_ref[span, :] = dot(hid_t[span, :], rows_ref[1]).astype(BF16)


def local(n, m, tokens, w_gate, w_up, w_down, grad_out):
    block, depth = tokens.shape
    ff = w_gate.shape[1]
    width = chunk_of(ff)
    steps = ff // width
    count = n * block
    half = count // 2
    vmem = pl.BlockSpec(memory_space=pltpu.VMEM)
    anywhere = pl.BlockSpec(memory_space=pl.ANY)
    dma = pltpu.SemaphoreType.DMA
    mixed, gtok, acts, rows = pl.pallas_call(
        functools.partial(main_kernel, n, m),
        out_shape=(
            jax.ShapeDtypeStruct((block, depth), BF16),
            jax.ShapeDtypeStruct((block, depth), BF16),
            jax.ShapeDtypeStruct((steps, 3, count, width), BF16),
            jax.ShapeDtypeStruct((2, count, depth), BF16),
        ),
        in_specs=[vmem, vmem, anywhere, anywhere, anywhere],
        out_specs=(vmem, vmem, vmem, vmem),
        scratch_shapes=[
            pltpu.VMEM((2, count, depth), BF16),
            pltpu.VMEM((steps, depth, width), BF16),
            pltpu.VMEM((steps, depth, width), BF16),
            pltpu.VMEM((steps, width, depth), BF16),
            pltpu.VMEM((3, count, width), F32),
            pltpu.VMEM((steps, 3, half, width), F32),
            pltpu.VMEM((steps, 3, half, width), BF16),
            pltpu.VMEM((steps, 3, half, width), BF16),
            pltpu.VMEM((steps, 3, half, width), BF16),
            pltpu.VMEM((steps, m - 1, 3, half, width), BF16),
            pltpu.VMEM((steps, 3, count, width), BF16),
            pltpu.VMEM((count, depth), F32),
            pltpu.VMEM((count, depth), F32),
            pltpu.VMEM((n, 2, block, depth), BF16),
            pltpu.VMEM((n, 2, block, depth), BF16),
            dma((steps, 3)),
            dma((2, n)),
            dma((2, n)),
            dma((steps, 2)),
            dma((steps, 2)),
            dma((steps, m, 2)),
            dma((steps, m, 2)),
            dma((steps, 2)),
            dma((steps, 2)),
            dma((n, 2)),
            dma((n, 2)),
        ],
        compiler_params=pltpu.CompilerParams(
            collective_id=0, has_side_effects=True, vmem_limit_bytes=VMEM_BYTES
        ),
    )(tokens, grad_out, w_gate, w_up, w_down)
    mixed, gtok, grad_gate, grad_up, grad_down = pl.pallas_call(
        outer_kernel,
        grid=(steps,),
        out_shape=(
            jax.ShapeDtypeStruct((block, depth), BF16),
            jax.ShapeDtypeStruct((block, depth), BF16),
            jax.ShapeDtypeStruct((depth, ff), BF16),
            jax.ShapeDtypeStruct((depth, ff), BF16),
            jax.ShapeDtypeStruct((ff, depth), BF16),
        ),
        in_specs=[
            pl.BlockSpec((1, 3, count, width), lambda k: (k, 0, 0, 0)),
            pl.BlockSpec((2, count, depth), lambda k: (0, 0, 0)),
            pl.BlockSpec((block, depth), lambda k: (0, 0)),
            pl.BlockSpec((block, depth), lambda k: (0, 0)),
        ],
        out_specs=(
            pl.BlockSpec((block, depth), lambda k: (0, 0)),
            pl.BlockSpec((block, depth), lambda k: (0, 0)),
            pl.BlockSpec((depth, width), lambda k: (0, k)),
            pl.BlockSpec((depth, width), lambda k: (0, k)),
            pl.BlockSpec((width, depth), lambda k: (k, 0)),
        ),
        scratch_shapes=[pltpu.VMEM((depth, count), BF16), pltpu.VMEM((width, count), BF16)],
        compiler_params=pltpu.CompilerParams(vmem_limit_bytes=VMEM_BYTES),
    )(acts, rows, mixed, gtok)
    return mixed, gtok, grad_gate, grad_up, grad_down


def solution(mesh):
    return jax.shard_map(
        functools.partial(local, mesh.shape["gx"], mesh.shape["gy"]),
        mesh=mesh,
        in_specs=(
            P(("grp", "gx"), ("gy", "gz")),
            P(("gy", "gz"), "gx"),
            P(("gy", "gz"), "gx"),
            P("gx", ("gy", "gz")),
            P(("grp", "gx"), ("gy", "gz")),
        ),
        out_specs=(
            P(("grp", "gx"), ("gy", "gz")),
            P(("grp", "gx"), ("gy", "gz")),
            P(("grp", "gy", "gz"), "gx"),
            P(("grp", "gy", "gz"), "gx"),
            P(("grp", "gx"), ("gy", "gz")),
        ),
        check_vma=False,
    )
```
